128 devices in a mesh: blk: 16 (over x_lo, y, core), layer: 8 (over z, x_hi).
Axes of the slice: x: 4 (x_hi: 2, x_lo: 2; x = x_hi * 2 + x_lo), y: 4, z: 4, core: 2. Of those that a mesh axis runs over, the one named last changes fastest.
Arguments:
- points: float32 [16384, 128], P('blk'), may hold values from -6 to 6
- inv_scale: float32 [128], replicated, may hold values from 0.01 to 0.25
- vectors: float32 [16384, 64], P('blk'), may hold values from -6 to 6
- noise: float32 [16384], P(('blk', 'layer')), may hold values from 0.1 to 1
Outputs:
- result: float32 [16384, 64], P(('blk', 'layer'))
The draws below stay inside these ranges and needn't reach their ends.
All inputs are finite; a program needn't handle non-finite values.
Results may differ from the reference program's by a relative error of at most 0.0001.
Values sent between devices are 32-bit elements; how exact they have to be, the bound alone decides.
No kernel may reach another device: no remote copies, remote signals or barrier semaphores. Data moves between devices by JAX's collectives and lax.ppermute only.
A program may use at most 64 MiB of HBM per device.

```python
import math
import jax
import jax.numpy as jnp
from jax import lax

FEATS = 128
RHS = 64
BLOCK = 1024
NPTS = 16384
N_BLK = 16
N_LAYER = 8


def shard_levels(stream_key, dims, pieces, low, top_value):
    gain, own = 1.0, jax.random.fold_in(stream_key, 6)
    for axis_at, blocks in pieces:
        draws = jnp.exp(jax.random.uniform(jax.random.fold_in(own, axis_at), (blocks,), jnp.float32, low / len(pieces), top_value / len(pieces)))
        gain = gain * jnp.repeat(draws, dims[axis_at] // blocks).reshape([-1 if axis == axis_at else 1 for axis in range(len(dims))])
    return gain


def centred(own_key, extent, deviation, reach, pieces=(), held_as=jnp.bfloat16):
    gain = shard_levels(own_key, extent, pieces, -0.22, 0.18) if pieces else 1.0
    result = jax.random.normal(own_key, extent, jnp.float32) * deviation * gain
    return jnp.minimum(jnp.maximum(result, -reach), reach).astype(held_as)


def setup_inputs(seed: int = 0) -> dict:
    key_of = jax.random.split(jax.random.key(seed), 5)
    return {
        "points": centred(key_of[0], (NPTS, FEATS), 1.0, 6.0, ((0, 16),), jnp.float32),
        "inv_scale": jnp.clip(jnp.exp(jax.random.uniform(key_of[1], (FEATS,), jnp.float32, math.log(0.01), math.log(0.25))), 0.01, 0.25),
        "vectors": centred(key_of[2], (NPTS, RHS), 1.0, 6.0, ((0, 16),), jnp.float32),
        "noise": jnp.clip(jnp.exp(math.log(1.0) - 2.3025851 * jax.random.uniform(key_of[3], (NPTS,), jnp.float32) ** shard_levels(key_of[3], (NPTS,), ((0, 128),), -0.2, 0.2)), 0.1, 1.0),
    }


ROOT_FIVE = 5.0 ** 0.5
FIVE_THIRDS = 5.0 / 3.0

def matern(left_scaled, right_scaled):
    left_norms = lax.optimization_barrier(jnp.sum(left_scaled * left_scaled, axis=1))
    right_norms = lax.optimization_barrier(jnp.sum(right_scaled * right_scaled, axis=1))
    cross = jnp.dot(left_scaled, right_scaled.T, precision=lax.Precision.HIGHEST, preferred_element_type=jnp.float32)
    distance_sq = jnp.maximum(left_norms[:, None] + right_norms[None, :] - 2.0 * cross, 0.0)
    radius = jnp.sqrt(distance_sq)
    return (1.0 + ROOT_FIVE * radius + FIVE_THIRDS * distance_sq) * jnp.exp(-ROOT_FIVE * radius)

def tile_pair(members):
    left_scaled, right_scaled, left_vectors, right_vectors = members
    kernel = matern(left_scaled, right_scaled)
    direct = jnp.dot(kernel, right_vectors, precision=lax.Precision.HIGHEST, preferred_element_type=jnp.float32)
    mirrored = jnp.dot(kernel.T, left_vectors, precision=lax.Precision.HIGHEST, preferred_element_type=jnp.float32)
    return (direct, mirrored)

def reference(points, inv_scale, vectors, noise):
    scaled = (points * inv_scale[None, :]).reshape(N_BLK, BLOCK, FEATS)
    grouped = vectors.reshape(N_BLK, BLOCK, RHS)
    summed = jnp.zeros((N_BLK, BLOCK, RHS), jnp.float32)
    for distance in range(N_LAYER):
        partner_scaled = jnp.roll(scaled, -distance, axis=0)
        partner_vectors = jnp.roll(grouped, -distance, axis=0)
        direct, mirrored = lax.map(tile_pair, (scaled, partner_scaled, grouped, partner_vectors))
        summed = summed + direct
        if distance > 0:
            summed = summed + jnp.roll(mirrored, distance, axis=0)
    normalizer = float(BLOCK * (2 * N_LAYER - 1)) ** (-0.5)
    return summed.reshape(NPTS, RHS) * normalizer + noise[:, None] * vectors
```

```python
import jax
import jax.numpy as jnp
from jax import lax
from jax.experimental import pallas as pl
from jax.experimental.pallas import tpu as pltpu
from jax.sharding import PartitionSpec as P

F32 = jnp.float32
BF16 = jnp.bfloat16
ROOT_THREE = 3.0**0.5
POINT_SCALE = (5.0 / 3.0) ** 0.5
EXP2_SCALE = -ROOT_THREE * 1.4426950408889634
TINY = 1e-30
LANES = 128
CHUNK = 256

SHIFTS = (1, 2, 7, 6, 3, 5, 4)
FIRST_GROUP = 3


def passed_along(value, axis, steps):
    count = lax.axis_size(axis)
    pairs = [(source, (source + steps) % count) for source in range(count)]
    return lax.ppermute(value, axis, pairs)


def two_parts(x):
    high = x.astype(BF16)
    return high, (x - high.astype(F32)).astype(BF16)


def three_parts(x):
    high = x.astype(BF16)
    rest = x - high.astype(F32)
    middle = rest.astype(BF16)
    return high, middle, (rest - middle.astype(F32)).astype(BF16)


def side_by_side(*parts):
    return jnp.concatenate(parts, axis=1)


def stacked(*parts):
    return jnp.concatenate(parts, axis=0)


def across(left, right):
    return lax.dot_general(left, right, (((1,), (1,)), ((), ())), preferred_element_type=F32)


def pair_kernel(count, final, with_total, *refs):
    inv_ref, points_ref, vectors_t_ref = refs[:3]
    pieces = refs[3 : 3 + count]
    rest = refs[3 + count :]
    if with_total:
        total_in, rest = rest[0], rest[1:]
    if final:
        direct_ref, mirrored_ref, total, left, left_norms, left_vectors = rest
    else:
        total, mirrored_ref, left, left_norms, left_vectors = rest
    rows, feats = points_ref.shape
    columns = vectors_t_ref.shape[0]
    inv = inv_ref[...] * POINT_SCALE
    x = points_ref[...] * inv
    left_norms[...] = jnp.broadcast_to(jnp.sum(x * x, axis=1, keepdims=True), (rows, LANES))
    high, middle, low = three_parts(x * (-2.0))
    for place, part in enumerate((high, middle, high, middle, high, low)):
        left[:, place * feats : (place + 1) * feats] = part
    high, low = two_parts(vectors_t_ref[...])
    left_vectors[:columns, :] = high
    left_vectors[columns:, :] = low
    zero = jnp.zeros((columns, CHUNK), BF16)
    for pair in range(count // 2):
        held = [pieces[2 * pair][...], pieces[2 * pair + 1][...]]
        y = stacked(held[0][:LANES], held[1][:LANES]) * inv
        right_norms = jnp.sum((y * y).T, axis=0, keepdims=True)
        high, middle, low = three_parts(y)
        right = side_by_side(high, high, middle, middle, low, high)
        high, low = two_parts(side_by_side(held[0][LANES:], held[1][LANES:]))
        right_vectors = side_by_side(
            stacked(high, low), stacked(high, jnp.zeros_like(high))
        )
        mirrored = jnp.zeros((2 * columns, 2 * LANES), F32)
        for chunk in range(rows // CHUNK):
            here = pl.ds(chunk * CHUNK, CHUNK)
            cross = across(left[here, :], right)
            norms = left_norms[here, :]
            square = jnp.maximum(cross + side_by_side(norms, norms) + right_norms, TINY)
            radius = square * lax.rsqrt(square)
            kernel = ((radius + ROOT_THREE) * radius + 1.0) * jnp.exp2(radius * EXP2_SCALE)
            high, low = two_parts(kernel)
            direct = across(side_by_side(high, low), right_vectors)
            if pair > 0:
                total[here, :] += direct
            elif with_total:
                total[here, :] = total_in[here, :] + direct
            else:
                total[here, :] = direct
            own = left_vectors[:columns, here]
            own_low = left_vectors[columns:, here]
            mirrored = mirrored + jnp.dot(
                stacked(side_by_side(own, own), side_by_side(own_low, zero)),
                stacked(high, low),
                preferred_element_type=F32,
            )
        mirrored = mirrored[:columns] + mirrored[columns:]
        mirrored_ref[2 * pair, :, :] = mirrored[:, :LANES]
        mirrored_ref[2 * pair + 1, :, :] = mirrored[:, LANES:]
    if final:
        for piece in range(rows // LANES):
            turned = total[piece * LANES : (piece + 1) * LANES, :].T
            direct_ref[piece, :, :] = turned[:columns] + turned[columns:]


def paired(inv, points, vectors_t, pieces, total=None, final=False):
    rows, feats = points.shape
    columns = vectors_t.shape[0]
    count = len(pieces)
    whole = pl.BlockSpec(memory_space=pltpu.VMEM)
    mirrored_shape = jax.ShapeDtypeStruct((count, columns, LANES), F32)
    total_shape = jax.ShapeDtypeStruct((rows, 2 * columns), F32)
    scratch = [
        pltpu.VMEM((rows, 6 * feats), BF16),
        pltpu.VMEM((rows, LANES), F32),
        pltpu.VMEM((2 * columns, rows), BF16),
    ]
    if final:
        out_shape = (
            jax.ShapeDtypeStruct((rows // LANES, columns, LANES), F32),
            mirrored_shape,
        )
        scratch = [pltpu.VMEM(total_shape.shape, F32)] + scratch
    else:
        out_shape = (total_shape, mirrored_shape)
    args = [inv, points, vectors_t, *pieces] + ([] if total is None else [total])

    def body(*refs):
        pair_kernel(count, final, total is not None, *refs)

    return pl.pallas_call(
        body,
        out_shape=out_shape,
        in_specs=[whole] * len(args),
        out_specs=(whole, whole),
        scratch_shapes=scratch,
        compiler_params=pltpu.CompilerParams(vmem_limit_bytes=32 * 1024 * 1024),
        cost_estimate=pl.CostEstimate(
            flops=2 * rows * LANES * count * (6 * feats + 8 * columns),
            bytes_accessed=4 * (rows * (feats + columns) + count * 2 * LANES * LANES),
            transcendentals=0,
        ),
    )(*args)


def per_device(points, inv_scale, vectors, noise):
    layers = lax.axis_size("layer")
    layer_index = lax.axis_index("layer")
    rows = points.shape[0]
    piece_rows = rows // layers
    inv = inv_scale[None, :]
    vectors_t = vectors.T
    own_points = lax.dynamic_slice_in_dim(points, layer_index * piece_rows, piece_rows, 0)
    own_vectors = lax.dynamic_slice_in_dim(vectors_t, layer_index * piece_rows, piece_rows, 1)
    own = stacked(own_points, own_vectors)
    arrived = [passed_along(own, "blk", -shift) for shift in SHIFTS]
    total, back_first = paired(inv, points, vectors_t, [own] + arrived[:FIRST_GROUP])
    direct, back_last = paired(
        inv, points, vectors_t, arrived[FIRST_GROUP:], total=total, final=True
    )
    back = [back_first[i + 1] for i in range(FIRST_GROUP)]
    back += [back_last[i] for i in range(len(SHIFTS) - FIRST_GROUP)]
    tiles = lax.all_to_all(direct, "layer", 0, 0, tiled=True)
    returned = [passed_along(part, "blk", shift) for part, shift in zip(back, SHIFTS)]
    own_sum = jnp.sum(tiles, axis=0)
    for part in returned:
        own_sum = own_sum + part
    normalizer = float(rows * (2 * layers - 1)) ** (-0.5)
    return (own_sum * normalizer + noise[None, :] * own_vectors).T


def solution(mesh):
    placed = (P("blk", None), P(), P("blk", None), P(("blk", "layer")))
    return jax.shard_map(
        per_device, mesh=mesh, in_specs=placed, out_specs=P(("blk", "layer"), None), check_vma=False
    )
```

```python
import jax
import jax.numpy as jnp
from jax import lax
from jax.experimental import pallas as pl
from jax.experimental.pallas import tpu as pltpu
from jax.sharding import PartitionSpec as P

F32 = jnp.float32
BF16 = jnp.bfloat16
ROOT_THREE = 3.0**0.5
POINT_SCALE = (5.0 / 3.0) ** 0.5
EXP2_SCALE = -ROOT_THREE * 1.4426950408889634
TINY = 1e-30
LANES = 128
CHUNK = 256
VMEM_BYTES = 32 * 1024 * 1024

STEPS = ((0, 2), (4, 1), (-3, -5), (7, 6))
PARTS = len(STEPS)


def moved(value, which, back):
    blocks, layers = lax.axis_size("blk"), lax.axis_size("layer")
    pairs = []
    for block in range(blocks):
        for layer in range(layers):
            step = STEPS[which][layer % 2]
            if step:
                source = block * layers + layer
                target = (block + step) % blocks * layers + layer
                pairs.append((target, source) if back else (source, target))
    return lax.ppermute(value, ("blk", "layer"), pairs)


def two_parts(x):
    high = x.astype(BF16)
    return high, (x - high.astype(F32)).astype(BF16)


def three_parts(x):
    high = x.astype(BF16)
    rest = x - high.astype(F32)
    middle = rest.astype(BF16)
    return high, middle, (rest - middle.astype(F32)).astype(BF16)


def side_by_side(*parts):
    return jnp.concatenate(parts, axis=1)


def stacked(*parts):
    return jnp.concatenate(parts, axis=0)


def across(left, right):
    return lax.dot_general(left, right, (((1,), (1,)), ((), ())), preferred_element_type=F32)


def local_call(
    body, outs, args, scratch=(), aliases=None, flops=0, moved_bytes=0,
    space=pltpu.VMEM,
):
    whole = pl.BlockSpec(memory_space=pltpu.VMEM)
    return pl.pallas_call(
        body,
        out_shape=tuple(jax.ShapeDtypeStruct(shape, kind) for shape, kind in outs),
        in_specs=[pl.BlockSpec(memory_space=space)] * len(args),
        out_specs=(whole,) * len(outs),
        scratch_shapes=list(scratch),
        input_output_aliases=aliases or {},
        compiler_params=pltpu.CompilerParams(vmem_limit_bytes=VMEM_BYTES),
        cost_estimate=pl.CostEstimate(flops=flops, bytes_accessed=moved_bytes, transcendentals=0),
    )(*(pltpu.with_memory_space_constraint(arg, space) for arg in args))


def prepare(points, inv, vectors_t, noise):
    rows, feats = points.shape
    columns = vectors_t.shape[0]
    part_rows = rows // PARTS

    def body(points_hbm, vectors_hbm, inv_hbm, noise_hbm, own_ref, x_ref, v_ref, term_ref, raw, inv_ref, noise_ref, sems):
        layer = lax.axis_index("layer")
        copies = [
            pltpu.make_async_copy(source, target, sems.at[which])
            for which, (source, target) in enumerate(
                ((points_hbm, raw), (inv_hbm, inv_ref), (vectors_hbm, v_ref), (noise_hbm, noise_ref))
            )
        ]
        for copy in copies:
            copy.start()
        copies[1].wait()
        inv_row = inv_ref[...] * POINT_SCALE
        copies[0].wait()
        start = pl.multiple_of(layer // 2 * part_rows, part_rows)
        own_ref[:part_rows, :] = raw[pl.ds(start, part_rows), :] * inv_row
        x_ref[...] = raw[...] * inv_row
        copies[2].wait()
        for half in range(part_rows // LANES):
            place = pl.multiple_of(start + half * LANES, LANES)
            own_ref[part_rows + half * columns : part_rows + (half + 1) * columns, :] = v_ref[
                :, pl.ds(place, LANES)
            ]
        copies[3].wait()
        place = pl.multiple_of(layer * LANES, LANES)
        term_ref[...] = v_ref[:, pl.ds(place, LANES)] * noise_ref[...]

    outs = (
        ((part_rows + part_rows // LANES * columns, feats), F32),
        ((rows, feats), F32),
        ((columns, rows), F32),
        ((columns, LANES), F32),
    )
    scratch = (
        pltpu.VMEM((rows, feats), F32),
        pltpu.VMEM((1, feats), F32),
        pltpu.VMEM((1, LANES), F32),
        pltpu.SemaphoreType.DMA((4,)),
    )
    return local_call(
        body, outs, (points, vectors_t, inv, noise), scratch, moved_bytes=2 << 20,
        space=pltpu.HBM,
    )


def load_right(held, columns):
    part_rows = 2 * LANES
    y = held[:part_rows]
    right_norms = jnp.sum((y * y).T, axis=0, keepdims=True)
    high, middle, low = three_parts(y)
    right = side_by_side(high, high, middle, middle, low, high)
    vectors = side_by_side(
        held[part_rows : part_rows + columns], held[part_rows + columns : part_rows + 2 * columns]
    )
    high, low = two_parts(vectors)
    right_vectors = side_by_side(stacked(high, low), stacked(high, jnp.zeros_like(high)))
    return right, right_norms, right_vectors


def tile(held, left, left_norms, left_vectors, total, add, mirrored_ref):
    rows = left.shape[0]
    columns = left_vectors.shape[0] // 2
    right, right_norms, right_vectors = load_right(held, columns)
    zero = jnp.zeros((columns, CHUNK), BF16)
    mirrored = jnp.zeros((2 * columns, 2 * LANES), F32)
    for chunk in range(rows // CHUNK):
        here = pl.ds(chunk * CHUNK, CHUNK)
        cross = across(left[here, :], right)
        norms = left_norms[here, :]
        square = jnp.maximum(cross + side_by_side(norms, norms) + right_norms, TINY)
        radius = square * lax.rsqrt(square)
        kernel = ((radius + ROOT_THREE) * radius + 1.0) * jnp.exp2(radius * EXP2_SCALE)
        high, low = two_parts(kernel)
        direct = across(side_by_side(high, low), right_vectors)
        if add:
            total[here, :] += direct
        else:
            total[here, :] = direct
        own = left_vectors[:columns, here]
        own_low = left_vectors[columns:, here]
        mirrored = mirrored + jnp.dot(
            stacked(side_by_side(own, own), side_by_side(own_low, zero)),
            stacked(high, low),
            preferred_element_type=F32,
        )
    mirrored = mirrored[:columns] + mirrored[columns:]
    mirrored_ref[:columns, :] = mirrored[:, :LANES]
    mirrored_ref[columns:, :] = mirrored[:, LANES:]


def tile_flops(rows, feats, columns):
    return 2 * rows * 2 * LANES * (6 * feats + 8 * columns)


def first_tile(x, vectors_t, own, piece):
    rows, feats = x.shape
    columns = vectors_t.shape[0]

    def body(x_ref, v_ref, own_ref, piece_ref, total, mirrored_ref, left, left_norms, left_vectors):
        x = x_ref[...]
        left_norms[...] = jnp.broadcast_to(jnp.sum(x * x, axis=1, keepdims=True), (rows, LANES))
        high, middle, low = three_parts(x * (-2.0))
        for place, part in enumerate((high, middle, high, middle, high, low)):
            left[:, place * feats : (place + 1) * feats] = part
        high, low = two_parts(v_ref[...])
        left_vectors[:columns, :] = high
        left_vectors[columns:, :] = low
        local = lax.axis_index("layer") % 2 == 0
        held = jnp.where(local, own_ref[...], piece_ref[...])
        tile(held, left, left_norms, left_vectors, total, False, mirrored_ref)

    outs = (
        ((rows, 2 * columns), F32),
        ((2 * columns, LANES), F32),
        ((rows, 6 * feats), BF16),
        ((rows, LANES), F32),
        ((2 * columns, rows), BF16),
    )
    return local_call(
        body, outs, (x, vectors_t, own, piece),
        flops=tile_flops(rows, feats, columns), moved_bytes=2 << 20,
    )


def next_tile(total, left, left_norms, left_vectors, piece, last):
    rows = left.shape[0]
    columns = left_vectors.shape[0] // 2
    feats = left.shape[1] // 6

    def plain(total_in, left, left_norms, left_vectors, piece_ref, total, mirrored_ref):
        tile(piece_ref[...], left, left_norms, left_vectors, total, True, mirrored_ref)

    def closing(total_in, left, left_norms, left_vectors, piece_ref, turned_ref, mirrored_ref, total):
        total[...] = total_in[...]
        tile(piece_ref[...], left, left_norms, left_vectors, total, True, mirrored_ref)
        for place in range(rows // LANES):
            turned = total[place * LANES : (place + 1) * LANES, :].T
            turned_ref[place, :, :] = turned[:columns] + turned[columns:]

    args = (total, left, left_norms, left_vectors, piece)
    cost = dict(flops=tile_flops(rows, feats, columns), moved_bytes=2 << 20)
    mirrored = ((2 * columns, LANES), F32)
    if last:
        outs = (((rows // LANES, columns, LANES), F32), mirrored)
        return local_call(closing, outs, args, (pltpu.VMEM((rows, 2 * columns), F32),), **cost)
    return local_call(plain, ((total.shape, F32), mirrored), args, aliases={0: 0}, **cost)


def joined(tiles, returned):
    columns = tiles.shape[1]

    def body(tiles_in, *refs):
        parts, tiles = refs[:-1], refs[-1]
        total = parts[0][...]
        for part in parts[1:]:
            total = total + part[...]
        tiles[...] = tiles_in[...]
        place = lax.axis_index("layer") // 2 * 2
        tiles[place, :, :] += total[:columns]
        tiles[place + 1, :, :] += total[columns:]

    return local_call(
        body, ((tiles.shape, F32),), (tiles, *returned), moved_bytes=1 << 19
    )[0]


def per_device(points, inv_scale, vectors, noise):
    layers = lax.axis_size("layer")
    rows = points.shape[0]
    own, x, vectors_t, noise_term = prepare(
        points, inv_scale[None, :], vectors.T, noise[None, :]
    )
    arrived = [moved(own, which, False) for which in range(PARTS)]
    total, back, left, left_norms, left_vectors = first_tile(x, vectors_t, own, arrived[0])
    returned = [moved(back, 0, True)]
    for which in range(1, PARTS):
        total, back = next_tile(
            total, left, left_norms, left_vectors, arrived[which], which == PARTS - 1
        )
        returned.append(moved(back, which, True))
    tiles = lax.all_to_all(joined(total, returned), "layer", 0, 0, tiled=True)
    normalizer = float(rows * (2 * layers - 1)) ** (-0.5)
    return (jnp.sum(tiles, axis=0) * normalizer + noise_term).T


def solution(mesh):
    placed = (P("blk", None), P(), P("blk", None), P(("blk", "layer")))
    return jax.shard_map(
        per_device, mesh=mesh, in_specs=placed, out_specs=P(("blk", "layer"), None), check_vma=False
    )
```

```python
import jax
import jax.numpy as jnp
from jax import lax
from jax.experimental import pallas as pl
from jax.experimental.pallas import tpu as pltpu
from jax.sharding import PartitionSpec as P

F32 = jnp.float32
BF16 = jnp.bfloat16
ROOT_THREE = 3.0**0.5
POINT_SCALE = (5.0 / 3.0) ** 0.5
EXP2_SCALE = -ROOT_THREE * 1.4426950408889634
TINY = 1e-30
LANES = 128
CHUNK = 256
VMEM_BYTES = 32 * 1024 * 1024

CHIP_STEPS = (-1, -2, 3)


def permuted(value, target_of):
    count = lax.axis_size("blk")
    pairs = [(block, target_of(block) % count) for block in range(count)]
    return lax.ppermute(value, "blk", pairs)


def swapped(value):
    return permuted(value, lambda block: block ^ 1)


def stepped(value, chips):
    return permuted(value, lambda block: block + 2 * chips)


def across_the_ring(value):
    count = lax.axis_size("blk")
    pairs = [(block, (block + count // 2) % count) for block in range(0, count, 2)]
    return lax.ppermute(value, "blk", pairs)


def two_parts(x):
    high = x.astype(BF16)
    return high, (x - high.astype(F32)).astype(BF16)


def three_parts(x):
    high = x.astype(BF16)
    rest = x - high.astype(F32)
    middle = rest.astype(BF16)
    return high, middle, (rest - middle.astype(F32)).astype(BF16)


def side_by_side(*parts):
    return jnp.concatenate(parts, axis=1)


def stacked(*parts):
    return jnp.concatenate(parts, axis=0)


def across(left, right):
    return lax.dot_general(left, right, (((1,), (1,)), ((), ())), preferred_element_type=F32)


def local_call(body, outs, args, scratch=(), aliases=None, macs=0, space=pltpu.VMEM):
    whole = pl.BlockSpec(memory_space=pltpu.VMEM)
    return pl.pallas_call(
        body,
        out_shape=tuple(jax.ShapeDtypeStruct(shape, kind) for shape, kind in outs),
        in_specs=[pl.BlockSpec(memory_space=space)] * len(args),
        out_specs=(whole,) * len(outs),
        scratch_shapes=list(scratch),
        input_output_aliases=aliases or {},
        compiler_params=pltpu.CompilerParams(vmem_limit_bytes=VMEM_BYTES),
        cost_estimate=pl.CostEstimate(flops=2 * macs, bytes_accessed=1 << 20, transcendentals=0),
    )(*(pltpu.with_memory_space_constraint(arg, space) for arg in args))


def prepare(points, inv, vectors_t, noise):
    rows, feats = points.shape
    columns = vectors_t.shape[0]
    tiles = rows // LANES

    def body(
        points_hbm, vectors_hbm, inv_hbm, noise_hbm, packed_ref, piece_ref, term_ref,
        raw, raw_vectors, inv_ref, noise_ref, sems,
    ):
        layer = lax.axis_index("layer")
        copies = [
            pltpu.make_async_copy(source, target, sems.at[which])
            for which, (source, target) in enumerate(
                (
                    (points_hbm, raw),
                    (inv_hbm, inv_ref),
                    (vectors_hbm, raw_vectors),
                    (noise_hbm, noise_ref),
                )
            )
        ]
        for copy in copies:
            copy.start()
        copies[1].wait()
        inv_row = inv_ref[...] * POINT_SCALE
        copies[0].wait()
        start = pl.multiple_of(layer * LANES, LANES)
        piece_ref[:LANES, :] = raw[pl.ds(start, LANES), :] * inv_row
        packed_ref[:rows, :] = raw[...] * inv_row
        copies[2].wait()
        for tile in range(tiles):
            packed_ref[rows + tile * columns : rows + (tile + 1) * columns, :] = raw_vectors[
                :, tile * LANES : (tile + 1) * LANES
            ]
        own_vectors = raw_vectors[:, pl.ds(start, LANES)]
        piece_ref[LANES:, :] = own_vectors
        copies[3].wait()
        term_ref[...] = own_vectors * noise_ref[...]

    outs = (
        ((rows + tiles * columns, feats), F32),
        ((LANES + columns, feats), F32),
        ((columns, LANES), F32),
    )
    scratch = (
        pltpu.VMEM((rows, feats), F32),
        pltpu.VMEM((columns, rows), F32),
        pltpu.VMEM((1, feats), F32),
        pltpu.VMEM((1, LANES), F32),
        pltpu.SemaphoreType.DMA((4,)),
    )
    return local_call(body, outs, (points, vectors_t, inv, noise), scratch, space=pltpu.HBM)


def load_left(packed, left, left_norms, left_vectors):
    rows = left.shape[0]
    columns = left_vectors.shape[0] // 2
    x = packed[:rows, :]
    left_norms[...] = jnp.broadcast_to(jnp.sum(x * x, axis=1, keepdims=True), (rows, LANES))
    high, middle, low = three_parts(x * (-2.0))
    feats = x.shape[1]
    for place, part in enumerate((high, middle, high, middle, high, low)):
        left[:, place * feats : (place + 1) * feats] = part
    for tile in range(rows // LANES):
        high, low = two_parts(packed[rows + tile * columns : rows + (tile + 1) * columns, :])
        left_vectors[:columns, tile * LANES : (tile + 1) * LANES] = high
        left_vectors[columns:, tile * LANES : (tile + 1) * LANES] = low


def load_right(pieces):
    held = [piece[...] for piece in pieces]
    y = stacked(*(piece[:LANES] for piece in held))
    right_norms = jnp.sum((y * y).T, axis=0, keepdims=True)
    high, middle, low = three_parts(y)
    right = side_by_side(high, high, middle, middle, low, high)
    high, low = two_parts(side_by_side(*(piece[LANES:] for piece in held)))
    right_vectors = side_by_side(stacked(high, low), stacked(high, jnp.zeros_like(high)))
    return right, right_norms, right_vectors


def tile_products(side, loaded, total_in, total, mirrored):
    left, left_norms, left_vectors = side
    right, right_norms, right_vectors = loaded
    rows = left.shape[0]
    columns = left_vectors.shape[0] // 2
    count = right.shape[0] // LANES
    zero = jnp.zeros((columns, CHUNK), BF16)
    for chunk in range(rows // CHUNK):
        here = pl.ds(chunk * CHUNK, CHUNK)
        cross = across(left[here, :], right)
        norms = left_norms[here, :]
        square = jnp.maximum(cross + side_by_side(*(norms,) * count) + right_norms, TINY)
        radius = square * lax.rsqrt(square)
        kernel = ((radius + ROOT_THREE) * radius + 1.0) * jnp.exp2(radius * EXP2_SCALE)
        high, low = two_parts(kernel)
        direct = across(side_by_side(high, low), right_vectors)
        total[here, :] = direct if total_in is None else total_in[here, :] + direct
        own = left_vectors[:columns, here]
        own_low = left_vectors[columns:, here]
        part = jnp.dot(
            stacked(side_by_side(own, own), side_by_side(own_low, zero)),
            stacked(high, low),
            preferred_element_type=F32,
        )
        mirrored = part if mirrored is None else mirrored + part
    return mirrored


def folded(mirrored):
    columns = mirrored.shape[0] // 2
    return mirrored[:columns] + mirrored[columns:]


def write_turned(total, turned_ref):
    columns = total.shape[1] // 2
    for place in range(turned_ref.shape[0]):
        turned = total[place * LANES : (place + 1) * LANES, :].T
        turned_ref[place, :, :] = turned[:columns] + turned[columns:]


def macs_of(rows, feats, columns, count):
    return rows * count * LANES * (6 * feats + 8 * columns)


def early_tiles(packed, other_packed, piece, arrived):
    feats = packed.shape[1]
    columns = piece.shape[0] - LANES
    rows = packed.shape[0] * LANES // (LANES + columns)

    def body(
        packed, other_packed, piece, arrived,
        total, left, norms, vectors, other_total, other_left, other_norms, other_vectors, back_ref,
    ):
        load_left(packed, left, norms, vectors)
        load_left(other_packed, other_left, other_norms, other_vectors)
        loaded = load_right((piece, arrived))
        mirrored = tile_products((left, norms, vectors), loaded, None, total, None)
        other = (other_left, other_norms, other_vectors)
        mirrored = tile_products(other, loaded, None, other_total, mirrored)
        back_ref[...] = folded(mirrored)[:, LANES:]

    side = (
        ((rows, 2 * columns), F32),
        ((rows, 6 * feats), BF16),
        ((rows, LANES), F32),
        ((2 * columns, rows), BF16),
    )
    outs = side + side + (((columns, LANES), F32),)
    args = (packed, other_packed, piece, arrived)
    out = local_call(body, outs, args, macs=macs_of(2 * rows, feats, columns, 2))
    return out[:4], out[4:8], out[8]


def other_tiles(side, pieces):
    total, left, norms, vectors = side
    rows, columns = left.shape[0], vectors.shape[0] // 2

    def body(total_in, left, norms, vectors, *refs):
        arrived, turned_ref, shared_ref, back_ref, total = refs[:3], *refs[3:]
        loaded = load_right(arrived)
        mirrored = tile_products((left, norms, vectors), loaded, total_in, total, None)
        shared_ref[...] = mirrored[:, : 2 * LANES]
        back_ref[...] = folded(mirrored[:, 2 * LANES :])
        write_turned(total, turned_ref)

    outs = (
        ((rows // LANES, columns, LANES), F32),
        ((2 * columns, 2 * LANES), F32),
        ((columns, LANES), F32),
    )
    scratch = (pltpu.VMEM((rows, 2 * columns), F32),)
    macs = macs_of(rows, left.shape[1] // 6, columns, 3)
    return local_call(body, outs, (total, left, norms, vectors, *pieces), scratch, macs=macs)


def own_tiles(side, shared, pieces):
    total, left, norms, vectors = side
    rows, columns = left.shape[0], vectors.shape[0] // 2

    def body(total_in, left, norms, vectors, shared_ref, *refs):
        arrived, turned_ref, first_ref, second_ref, total = refs[:2], *refs[2:]
        loaded = load_right(arrived)
        mirrored = tile_products((left, norms, vectors), loaded, total_in, total, shared_ref[...])
        mirrored = folded(mirrored)
        first_ref[...] = mirrored[:, :LANES]
        second_ref[...] = mirrored[:, LANES:]
        write_turned(total, turned_ref)

    back = ((columns, LANES), F32)
    outs = (((rows // LANES, columns, LANES), F32), back, back)
    scratch = (pltpu.VMEM((rows, 2 * columns), F32),)
    macs = macs_of(rows, left.shape[1] // 6, columns, 2)
    return local_call(body, outs, (total, left, norms, vectors, shared, *pieces), scratch, macs=macs)


def per_device(points, inv_scale, vectors, noise):
    layers = lax.axis_size("layer")
    rows = points.shape[0]
    packed, piece, noise_term = prepare(points, inv_scale[None, :], vectors.T, noise[None, :])
    near, middle, far = CHIP_STEPS
    near_piece = stepped(piece, near)
    other_packed = swapped(packed)
    middle_piece = stepped(piece, middle)
    far_piece = stepped(piece, far)
    ring_piece = across_the_ring(piece)
    own, other, near_back = early_tiles(packed, other_packed, piece, near_piece)
    near_back = stepped(near_back, -near)
    for_other, shared, ring_back = other_tiles(other, (middle_piece, far_piece, ring_piece))
    from_other = swapped(for_other)
    direct, middle_back, far_back = own_tiles(own, shared, (middle_piece, far_piece))
    tiles = lax.all_to_all(direct + from_other, "layer", 0, 0, tiled=True)
    returned = (
        near_back
        + across_the_ring(ring_back)
        + stepped(middle_back, -middle)
        + stepped(far_back, -far)
    )
    normalizer = float(rows * (2 * layers - 1)) ** (-0.5)
    return ((jnp.sum(tiles, axis=0) + returned) * normalizer + noise_term).T


def solution(mesh):
    placed = (P("blk", None), P(), P("blk", None), P(("blk", "layer")))
    return jax.shard_map(
        per_device, mesh=mesh, in_specs=placed, out_specs=P(("blk", "layer"), None), check_vma=False
    )
```

```python
import jax
import jax.numpy as jnp
from jax import lax
from jax.experimental import pallas as pl
from jax.experimental.pallas import tpu as pltpu
from jax.sharding import PartitionSpec as P

F32 = jnp.float32
BF16 = jnp.bfloat16
ROOT_THREE = 3.0**0.5
POINT_SCALE = (5.0 / 3.0) ** 0.5
EXP2_SCALE = -ROOT_THREE * 1.4426950408889634
TINY = 1e-30
LANES = 128
CHUNK = 256
VMEM_BYTES = 32 * 1024 * 1024

CHIP_STEPS = (-1, -2, 3)


def permuted(value, target_of):
    count = lax.axis_size("blk")
    pairs = [(block, target_of(block) % count) for block in range(count)]
    return lax.ppermute(value, "blk", pairs)


def swapped(value):
    return permuted(value, lambda block: block ^ 1)


def stepped(value, chips):
    return permuted(value, lambda block: block + 2 * chips)


def across_the_ring(value):
    count = lax.axis_size("blk")
    return permuted(value, lambda block: block + count // 2)


def two_parts(x):
    high = x.astype(BF16)
    return high, (x - high.astype(F32)).astype(BF16)


def three_parts(x):
    high = x.astype(BF16)
    rest = x - high.astype(F32)
    middle = rest.astype(BF16)
    return high, middle, (rest - middle.astype(F32)).astype(BF16)


def side_by_side(*parts):
    return jnp.concatenate(parts, axis=1)


def stacked(*parts):
    return jnp.concatenate(parts, axis=0)


def across(left, right):
    return lax.dot_general(left, right, (((1,), (1,)), ((), ())), preferred_element_type=F32)


def local_call(body, outs, args, scratch=(), aliases=None, macs=0, space=pltpu.VMEM):
    whole = pl.BlockSpec(memory_space=pltpu.VMEM)
    return pl.pallas_call(
        body,
        out_shape=tuple(jax.ShapeDtypeStruct(shape, kind) for shape, kind in outs),
        in_specs=[pl.BlockSpec(memory_space=space)] * len(args),
        out_specs=(whole,) * len(outs),
        scratch_shapes=list(scratch),
        input_output_aliases=aliases or {},
        compiler_params=pltpu.CompilerParams(vmem_limit_bytes=VMEM_BYTES),
        cost_estimate=pl.CostEstimate(flops=2 * macs, bytes_accessed=1 << 20, transcendentals=0),
    )(*(pltpu.with_memory_space_constraint(arg, space) for arg in args))


def prepare(points, inv, vectors_t, noise):
    rows, feats = points.shape
    columns = vectors_t.shape[0]
    tiles = rows // LANES

    def body(
        points_hbm, vectors_hbm, inv_hbm, noise_hbm, packed_ref, piece_ref, term_ref,
        raw, raw_vectors, inv_ref, noise_ref, sems,
    ):
        layer = lax.axis_index("layer")
        copies = [
            pltpu.make_async_copy(source, target, sems.at[which])
            for which, (source, target) in enumerate(
                (
                    (points_hbm, raw),
                    (inv_hbm, inv_ref),
                    (vectors_hbm, raw_vectors),
                    (noise_hbm, noise_ref),
                )
            )
        ]
        for copy in copies:
            copy.start()
        copies[1].wait()
        inv_row = inv_ref[...] * POINT_SCALE
        copies[0].wait()
        start = pl.multiple_of(layer * LANES, LANES)
        piece_ref[:LANES, :] = raw[pl.ds(start, LANES), :] * inv_row
        packed_ref[:rows, :] = raw[...] * inv_row
        copies[2].wait()
        for tile in range(tiles):
            packed_ref[rows + tile * columns : rows + (tile + 1) * columns, :] = raw_vectors[
                :, tile * LANES : (tile + 1) * LANES
            ]
        own_vectors = raw_vectors[:, pl.ds(start, LANES)]
        piece_ref[LANES:, :] = own_vectors
        copies[3].wait()
        term_ref[...] = own_vectors * noise_ref[...]

    outs = (
        ((rows + tiles * columns, feats), F32),
        ((LANES + columns, feats), F32),
        ((columns, LANES), F32),
    )
    scratch = (
        pltpu.VMEM((rows, feats), F32),
        pltpu.VMEM((columns, rows), F32),
        pltpu.VMEM((1, feats), F32),
        pltpu.VMEM((1, LANES), F32),
        pltpu.SemaphoreType.DMA((4,)),
    )
    return local_call(body, outs, (points, vectors_t, inv, noise), scratch, space=pltpu.HBM)


def load_left(packed, left, left_norms, left_vectors):
    rows = left.shape[0]
    columns = left_vectors.shape[0] // 2
    x = packed[:rows, :]
    left_norms[...] = jnp.broadcast_to(jnp.sum(x * x, axis=1, keepdims=True), (rows, LANES))
    high, middle, low = three_parts(x * (-2.0))
    feats = x.shape[1]
    for place, part in enumerate((high, middle, high, middle, high, low)):
        left[:, place * feats : (place + 1) * feats] = part
    for tile in range(rows // LANES):
        high, low = two_parts(packed[rows + tile * columns : rows + (tile + 1) * columns, :])
        left_vectors[:columns, tile * LANES : (tile + 1) * LANES] = high
        left_vectors[columns:, tile * LANES : (tile + 1) * LANES] = low


def load_right(pieces):
    held = [piece[...] for piece in pieces]
    y = stacked(*(piece[:LANES] for piece in held))
    right_norms = jnp.sum((y * y).T, axis=0, keepdims=True)
    high, middle, low = three_parts(y)
    right = side_by_side(high, high, middle, middle, low, high)
    high, low = two_parts(side_by_side(*(piece[LANES:] for piece in held)))
    right_vectors = side_by_side(stacked(high, low), stacked(high, jnp.zeros_like(high)))
    return right, right_norms, right_vectors


def tile_products(side, loaded, total_in, total, mirrored, both=True):
    left, left_norms, left_vectors = side
    right, right_norms, right_vectors = loaded
    rows = left.shape[0]
    columns = left_vectors.shape[0] // 2
    count = right.shape[0] // LANES
    zero = jnp.zeros((columns, CHUNK), BF16)
    for chunk in range(rows // CHUNK):
        here = pl.ds(chunk * CHUNK, CHUNK)
        cross = across(left[here, :], right)
        norms = left_norms[here, :]
        square = jnp.maximum(cross + side_by_side(*(norms,) * count) + right_norms, TINY)
        radius = square * lax.rsqrt(square)
        kernel = ((radius + ROOT_THREE) * radius + 1.0) * jnp.exp2(radius * EXP2_SCALE)
        high, low = two_parts(kernel)
        direct = across(side_by_side(high, low), right_vectors)
        total[here, :] = direct if total_in is None else total_in[here, :] + direct
        if not both:
            continue
        own = left_vectors[:columns, here]
        own_low = left_vectors[columns:, here]
        part = jnp.dot(
            stacked(side_by_side(own, own), side_by_side(own_low, zero)),
            stacked(high, low),
            preferred_element_type=F32,
        )
        mirrored = part if mirrored is None else mirrored + part
    return mirrored


def folded(mirrored):
    columns = mirrored.shape[0] // 2
    return mirrored[:columns] + mirrored[columns:]


def write_turned(total, turned_ref):
    columns = total.shape[1] // 2
    for place in range(turned_ref.shape[0]):
        turned = total[place * LANES : (place + 1) * LANES, :].T
        turned_ref[place, :, :] = turned[:columns] + turned[columns:]


def macs_of(rows, feats, columns, count):
    return rows * count * LANES * (6 * feats + 8 * columns)


def side_shapes(rows, feats, columns):
    return (
        ((rows, 2 * columns), F32),
        ((rows, 6 * feats), BF16),
        ((rows, LANES), F32),
        ((2 * columns, rows), BF16),
    )


def early_tiles(packed, other_packed, piece, arrived):
    feats = packed.shape[1]
    columns = piece.shape[0] - LANES
    rows = packed.shape[0] * LANES // (LANES + columns)

    def body(
        packed, other_packed, piece, arrived,
        total, left, norms, vectors, other_total, other_left, other_norms, other_vectors,
        back_ref, again_ref,
    ):
        again_ref[...] = piece[...]
        load_left(packed, left, norms, vectors)
        load_left(other_packed, other_left, other_norms, other_vectors)
        loaded = load_right((piece, arrived))
        mirrored = tile_products((left, norms, vectors), loaded, None, total, None)
        other = (other_left, other_norms, other_vectors)
        mirrored = tile_products(other, loaded, None, other_total, mirrored)
        back_ref[...] = folded(mirrored)[:, LANES:]

    side = side_shapes(rows, feats, columns)
    outs = side + side + (((columns, LANES), F32), (piece.shape, F32))
    args = (packed, other_packed, piece, arrived)
    out = local_call(body, outs, args, macs=macs_of(2 * rows, feats, columns, 2))
    return out[:4], out[4:8], out[8], out[9]


def later_tiles(side, other_side, pieces):
    rows, columns = side[1].shape[0], side[3].shape[0] // 2

    def body(total_in, left, norms, vectors, other_in, other_left, other_norms, other_vectors, *refs):
        arrived, total, other_total, first_ref, second_ref = refs[:2], *refs[2:]
        loaded = load_right(arrived)
        mirrored = tile_products((left, norms, vectors), loaded, total_in, total, None)
        other = (other_left, other_norms, other_vectors)
        mirrored = tile_products(other, loaded, other_in, other_total, mirrored)
        mirrored = folded(mirrored)
        first_ref[...] = mirrored[:, :LANES]
        second_ref[...] = mirrored[:, LANES:]

    total_shape = ((rows, 2 * columns), F32)
    back = ((columns, LANES), F32)
    outs = (total_shape, total_shape, back, back)
    macs = macs_of(2 * rows, side[1].shape[1] // 6, columns, 2)
    return local_call(body, outs, (*side, *other_side, *pieces), macs=macs)


def ring_tiles(side, piece):
    total, left, norms, vectors = side
    rows, columns = left.shape[0], vectors.shape[0] // 2

    def body(total_in, left, norms, vectors, piece, turned_ref, total):
        loaded = load_right((piece,))
        tile_products((left, norms, vectors), loaded, total_in, total, None, both=False)
        write_turned(total, turned_ref)

    outs = (((rows // LANES, columns, LANES), F32),)
    scratch = (pltpu.VMEM((rows, 2 * columns), F32),)
    macs = macs_of(rows, left.shape[1] // 6, columns, 1)
    return local_call(body, outs, (total, left, norms, vectors, piece), scratch, macs=macs)[0]


def joined(total, from_other, returned):
    def body(total, from_other, *refs):
        parts, tiles = refs[:-1], refs[-1]
        write_turned(total, tiles)
        tiles[...] += from_other[...]
        layer = lax.axis_index("layer")
        returned = parts[0][...]
        for part in parts[1:]:
            returned = returned + part[...]
        tiles[layer, :, :] += returned

    return local_call(body, ((from_other.shape, F32),), (total, from_other, *returned))[0]


def per_device(points, inv_scale, vectors, noise):
    layers = lax.axis_size("layer")
    rows = points.shape[0]
    packed, piece, noise_term = prepare(points, inv_scale[None, :], vectors.T, noise[None, :])
    near, middle, far = CHIP_STEPS
    near_piece = stepped(piece, near)
    other_packed = swapped(packed)
    middle_piece = stepped(piece, middle)
    far_piece = stepped(piece, far)
    own, other, near_back, piece = early_tiles(packed, other_packed, piece, near_piece)
    ring_piece = across_the_ring(piece)
    near_back = stepped(near_back, -near)
    total, other_total, middle_back, far_back = later_tiles(own, other, (middle_piece, far_piece))
    returned = (near_back, stepped(middle_back, -middle), stepped(far_back, -far))
    from_other = swapped(ring_tiles((other_total, *other[1:]), ring_piece))
    tiles = lax.all_to_all(joined(total, from_other, returned), "layer", 0, 0, tiled=True)
    normalizer = float(rows * (2 * layers - 1)) ** (-0.5)
    return (jnp.sum(tiles, axis=0) * normalizer + noise_term).T


def solution(mesh):
    placed = (P("blk", None), P(), P("blk", None), P(("blk", "layer")))
    return jax.shard_map(
        per_device, mesh=mesh, in_specs=placed, out_specs=P(("blk", "layer"), None), check_vma=False
    )
```

```python
import jax
import jax.numpy as jnp
from jax import lax
from jax.experimental import pallas as pl
from jax.experimental.pallas import tpu as pltpu
from jax.sharding import PartitionSpec as P

F32 = jnp.float32
BF16 = jnp.bfloat16
ROOT_THREE = 3.0**0.5
POINT_SCALE = (5.0 / 3.0) ** 0.5
EXP2_SCALE = -ROOT_THREE * 1.4426950408889634
TINY = 1e-30
LANES = 128
CHUNK = 256
VMEM_BYTES = 32 * 1024 * 1024

CHIP_STEPS = (-1, -2, 3)


def permuted(value, target_of):
    count = lax.axis_size("blk")
    pairs = [(block, target_of(block) % count) for block in range(count)]
    return lax.ppermute(value, "blk", pairs)


def swapped(value):
    return permuted(value, lambda block: block ^ 1)


def stepped(value, chips):
    return permuted(value, lambda block: block + 2 * chips)


def across_the_ring(value):
    count = lax.axis_size("blk")
    return permuted(value, lambda block: block + count // 2)


def two_parts(x):
    high = x.astype(BF16)
    return high, (x - high.astype(F32)).astype(BF16)


def three_parts(x):
    high = x.astype(BF16)
    rest = x - high.astype(F32)
    middle = rest.astype(BF16)
    return high, middle, (rest - middle.astype(F32)).astype(BF16)


def side_by_side(*parts):
    return jnp.concatenate(parts, axis=1)


def stacked(*parts):
    return jnp.concatenate(parts, axis=0)


def across(left, right):
    return lax.dot_general(left, right, (((1,), (1,)), ((), ())), preferred_element_type=F32)


def local_call(body, outs, args, scratch=(), aliases=None, macs=0, space=pltpu.VMEM):
    whole = pl.BlockSpec(memory_space=pltpu.VMEM)
    return pl.pallas_call(
        body,
        out_shape=tuple(jax.ShapeDtypeStruct(shape, kind) for shape, kind in outs),
        in_specs=[pl.BlockSpec(memory_space=space)] * len(args),
        out_specs=(whole,) * len(outs),
        scratch_shapes=list(scratch),
        input_output_aliases=aliases or {},
        compiler_params=pltpu.CompilerParams(vmem_limit_bytes=VMEM_BYTES),
        cost_estimate=pl.CostEstimate(flops=2 * macs, bytes_accessed=1 << 20, transcendentals=0),
    )(*(pltpu.with_memory_space_constraint(arg, space) for arg in args))


def prepare(points, inv, vectors_t, noise):
    rows, feats = points.shape
    columns = vectors_t.shape[0]
    tiles = rows // LANES

    def body(
        points_hbm, vectors_hbm, inv_hbm, noise_hbm, packed_ref, piece_ref, term_ref,
        raw, raw_vectors, inv_ref, noise_ref, sems,
    ):
        layer = lax.axis_index("layer")
        copies = [
            pltpu.make_async_copy(source, target, sems.at[which])
            for which, (source, target) in enumerate(
                (
                    (points_hbm, raw),
                    (inv_hbm, inv_ref),
                    (vectors_hbm, raw_vectors),
                    (noise_hbm, noise_ref),
                )
            )
        ]
        for copy in copies:
            copy.start()
        copies[1].wait()
        inv_row = inv_ref[...] * POINT_SCALE
        copies[0].wait()
        start = pl.multiple_of(layer * LANES, LANES)
        piece_ref[:LANES, :] = raw[pl.ds(start, LANES), :] * inv_row
        packed_ref[:rows, :] = raw[...] * inv_row
        copies[2].wait()
        for tile in range(tiles):
            packed_ref[rows + tile * columns : rows + (tile + 1) * columns, :] = raw_vectors[
                :, tile * LANES : (tile + 1) * LANES
            ]
        own_vectors = raw_vectors[:, pl.ds(start, LANES)]
        piece_ref[LANES:, :] = own_vectors
        copies[3].wait()
        term_ref[...] = own_vectors * noise_ref[...]

    outs = (
        ((rows + tiles * columns, feats), F32),
        ((LANES + columns, feats), F32),
        ((columns, LANES), F32),
    )
    scratch = (
        pltpu.VMEM((rows, feats), F32),
        pltpu.VMEM((columns, rows), F32),
        pltpu.VMEM((1, feats), F32),
        pltpu.VMEM((1, LANES), F32),
        pltpu.SemaphoreType.DMA((4,)),
    )
    return local_call(body, outs, (points, vectors_t, inv, noise), scratch, space=pltpu.HBM)


def load_left(packed, left, left_norms, left_vectors):
    rows = left.shape[0]
    columns = left_vectors.shape[0] // 2
    x = packed[:rows, :]
    left_norms[...] = jnp.broadcast_to(jnp.sum(x * x, axis=1, keepdims=True), (rows, LANES))
    high, middle, low = three_parts(x * (-2.0))
    feats = x.shape[1]
    for place, part in enumerate((high, middle, high, middle, high, low)):
        left[:, place * feats : (place + 1) * feats] = part
    for tile in range(rows // LANES):
        high, low = two_parts(packed[rows + tile * columns : rows + (tile + 1) * columns, :])
        left_vectors[:columns, tile * LANES : (tile + 1) * LANES] = high
        left_vectors[columns:, tile * LANES : (tile + 1) * LANES] = low


def load_right(pieces):
    held = [piece[...] for piece in pieces]
    y = stacked(*(piece[:LANES] for piece in held))
    right_norms = jnp.sum((y * y).T, axis=0, keepdims=True)
    high, middle, low = three_parts(y)
    right = side_by_side(high, high, middle, middle, low, high)
    high, low = two_parts(side_by_side(*(piece[LANES:] for piece in held)))
    right_vectors = side_by_side(stacked(high, low), stacked(high, jnp.zeros_like(high)))
    return right, right_norms, right_vectors


def tile_products(side, loaded, total_in, total, mirrored, backs):
    left, left_norms, left_vectors = side
    right, right_norms, right_vectors = loaded
    rows = left.shape[0]
    columns = left_vectors.shape[0] // 2
    count = right.shape[0] // LANES
    zero = jnp.zeros((columns, CHUNK), BF16)
    for chunk in range(rows // CHUNK):
        here = pl.ds(chunk * CHUNK, CHUNK)
        cross = across(left[here, :], right)
        norms = left_norms[here, :]
        square = jnp.maximum(cross + side_by_side(*(norms,) * count) + right_norms, TINY)
        radius = square * lax.rsqrt(square)
        kernel = ((radius + ROOT_THREE) * radius + 1.0) * jnp.exp2(radius * EXP2_SCALE)
        high, low = two_parts(kernel)
        direct = across(side_by_side(high, low), right_vectors)
        total[here, :] = direct if total_in is None else total_in[here, :] + direct
        if backs == 0:
            continue
        wide = backs * LANES
        own = left_vectors[:columns, here]
        own_low = left_vectors[columns:, here]
        part = jnp.dot(
            stacked(side_by_side(own, own), side_by_side(own_low, zero)),
            stacked(high[:, :wide], low[:, :wide]),
            preferred_element_type=F32,
        )
        mirrored = part if mirrored is None else mirrored + part
    return mirrored


def folded(mirrored):
    columns = mirrored.shape[0] // 2
    return mirrored[:columns] + mirrored[columns:]


def write_turned(total, turned_ref):
    columns = total.shape[1] // 2
    for place in range(turned_ref.shape[0]):
        turned = total[place * LANES : (place + 1) * LANES, :].T
        turned_ref[place, :, :] = turned[:columns] + turned[columns:]


def macs_of(rows, feats, columns, count):
    return rows * count * LANES * (6 * feats + 8 * columns)


def side_shapes(rows, feats, columns):
    return (
        ((rows, 2 * columns), F32),
        ((rows, 6 * feats), BF16),
        ((rows, LANES), F32),
        ((2 * columns, rows), BF16),
    )


def first_tiles(packed, other_packed, piece):
    feats = packed.shape[1]
    columns = piece.shape[0] - LANES
    rows = packed.shape[0] * LANES // (LANES + columns)

    def body(packed, other_packed, piece, *refs):
        own, other, again_ref = refs[:4], refs[4:8], refs[8]
        again_ref[...] = piece[...]
        loaded = load_right((piece,))
        for source, (total, *side) in ((packed, own), (other_packed, other)):
            load_left(source, *side)
            tile_products(side, loaded, None, total, None, 0)

    side = side_shapes(rows, feats, columns)
    outs = side + side + ((piece.shape, F32),)
    macs = macs_of(2 * rows, feats, columns, 1)
    out = local_call(body, outs, (packed, other_packed, piece), macs=macs)
    return out[:4], out[4:8], out[8]


def shared_tiles(own, other, pieces):
    rows, columns = own[1].shape[0], own[3].shape[0] // 2

    def body(*refs):
        (own_in, *own_side), (other_in, *other_side) = refs[:4], refs[4:8]
        arrived, total, other_total, first_ref, second_ref = refs[8:10], *refs[10:]
        loaded = load_right(arrived)
        mirrored = tile_products(own_side, loaded, own_in, total, None, 2)
        mirrored = tile_products(other_side, loaded, other_in, other_total, mirrored, 2)
        mirrored = folded(mirrored)
        first_ref[...] = mirrored[:, :LANES]
        second_ref[...] = mirrored[:, LANES:]

    total_shape = ((rows, 2 * columns), F32)
    back = ((columns, LANES), F32)
    outs = (total_shape, total_shape, back, back)
    macs = macs_of(2 * rows, own[1].shape[1] // 6, columns, 2)
    return local_call(body, outs, (*own, *other, *pieces), macs=macs)


def other_tiles(side, pieces):
    rows, columns = side[1].shape[0], side[3].shape[0] // 2

    def body(*refs):
        (total_in, *side), arrived, turned_ref, part_ref, total = refs[:4], refs[4:6], *refs[6:]
        part_ref[...] = tile_products(side, load_right(arrived), total_in, total, None, 1)
        write_turned(total, turned_ref)

    outs = (((rows // LANES, columns, LANES), F32), ((2 * columns, LANES), F32))
    scratch = (pltpu.VMEM((rows, 2 * columns), F32),)
    macs = macs_of(rows, side[1].shape[1] // 6, columns, 2)
    return local_call(body, outs, (*side, *pieces), scratch, macs=macs)


def own_tiles(side, part, piece):
    rows, columns = side[1].shape[0], side[3].shape[0] // 2

    def body(*refs):
        (total_in, *side), part_ref, arrived, total, back_ref = refs[:4], *refs[4:]
        loaded = load_right((arrived,))
        back_ref[...] = folded(tile_products(side, loaded, total_in, total, part_ref[...], 1))

    outs = (((rows, 2 * columns), F32), ((columns, LANES), F32))
    macs = macs_of(rows, side[1].shape[1] // 6, columns, 1)
    return local_call(body, outs, (*side, part, piece), macs=macs)


def joined(total, from_other):
    def body(total, from_other, tiles):
        write_turned(total, tiles)
        tiles[...] += from_other[...]

    return local_call(body, ((from_other.shape, F32),), (total, from_other))[0]


def per_device(points, inv_scale, vectors, noise):
    layers = lax.axis_size("layer")
    rows = points.shape[0]
    packed, piece, noise_term = prepare(points, inv_scale[None, :], vectors.T, noise[None, :])
    near, middle, far = CHIP_STEPS
    near_piece = stepped(piece, near)
    other_packed = swapped(packed)
    middle_piece = stepped(piece, middle)
    far_piece = stepped(piece, far)
    own, other, piece = first_tiles(packed, other_packed, piece)
    ring_piece = across_the_ring(piece)
    total, other_total, near_back, middle_back = shared_tiles(
        own, other, (near_piece, middle_piece)
    )
    for_other, part = other_tiles((other_total, *other[1:]), (far_piece, ring_piece))
    from_other = swapped(for_other)
    total, far_back = own_tiles((total, *own[1:]), part, far_piece)
    tiles = lax.all_to_all(joined(total, from_other), "layer", 0, 0, tiled=True)
    returned = (
        stepped(near_back, -near) + stepped(middle_back, -middle) + stepped(far_back, -far)
    )
    normalizer = float(rows * (2 * layers - 1)) ** (-0.5)
    return ((jnp.sum(tiles, axis=0) + returned) * normalizer + noise_term).T


def solution(mesh):
    placed = (P("blk", None), P(), P("blk", None), P(("blk", "layer")))
    return jax.shard_map(
        per_device, mesh=mesh, in_specs=placed, out_specs=P(("blk", "layer"), None), check_vma=False
    )
```

```python
import jax
import jax.numpy as jnp
from jax import lax
from jax.experimental import pallas as pl
from jax.experimental.pallas import tpu as pltpu
from jax.sharding import PartitionSpec as P

F32 = jnp.float32
BF16 = jnp.bfloat16
ROOT_THREE = 3.0**0.5
POINT_SCALE = (5.0 / 3.0) ** 0.5
EXP2_SCALE = -ROOT_THREE * 1.4426950408889634
TINY = 1e-30
LANES = 128
CHUNK = 256
VMEM_BYTES = 32 * 1024 * 1024

CHIP_STEPS = (-1, -2, 3)


def permuted(value, target_of):
    count = lax.axis_size("blk")
    pairs = [(block, target_of(block) % count) for block in range(count)]
    return lax.ppermute(value, "blk", pairs)


def swapped(value):
    return permuted(value, lambda block: block ^ 1)


def stepped(value, chips):
    return permuted(value, lambda block: block + 2 * chips)


def across_the_ring(value):
    count = lax.axis_size("blk")
    return permuted(value, lambda block: block + count // 2)


def two_parts(x):
    high = x.astype(BF16)
    return high, (x - high.astype(F32)).astype(BF16)


def three_parts(x):
    high = x.astype(BF16)
    rest = x - high.astype(F32)
    middle = rest.astype(BF16)
    return high, middle, (rest - middle.astype(F32)).astype(BF16)


def side_by_side(*parts):
    return jnp.concatenate(parts, axis=1)


def stacked(*parts):
    return jnp.concatenate(parts, axis=0)


def across(left, right):
    return lax.dot_general(left, right, (((1,), (1,)), ((), ())), preferred_element_type=F32)


def local_call(body, outs, args, scratch=(), aliases=None, macs=0, space=pltpu.VMEM):
    whole = pl.BlockSpec(memory_space=pltpu.VMEM)
    return pl.pallas_call(
        body,
        out_shape=tuple(jax.ShapeDtypeStruct(shape, kind) for shape, kind in outs),
        in_specs=[pl.BlockSpec(memory_space=space)] * len(args),
        out_specs=(whole,) * len(outs),
        scratch_shapes=list(scratch),
        input_output_aliases=aliases or {},
        compiler_params=pltpu.CompilerParams(vmem_limit_bytes=VMEM_BYTES),
        cost_estimate=pl.CostEstimate(flops=2 * macs, bytes_accessed=1 << 20, transcendentals=0),
    )(*(pltpu.with_memory_space_constraint(arg, space) for arg in args))


def prepare(points, inv, vectors_t, noise):
    rows, feats = points.shape
    columns = vectors_t.shape[0]
    tiles = rows // LANES

    def body(
        points_hbm, vectors_hbm, inv_hbm, noise_hbm, packed_ref, piece_ref, term_ref,
        raw, raw_vectors, inv_ref, noise_ref, sems,
    ):
        layer = lax.axis_index("layer")
        copies = [
            pltpu.make_async_copy(source, target, sems.at[which])
            for which, (source, target) in enumerate(
                (
                    (points_hbm, raw),
                    (inv_hbm, inv_ref),
                    (vectors_hbm, raw_vectors),
                    (noise_hbm, noise_ref),
                )
            )
        ]
        for copy in copies:
            copy.start()
        copies[1].wait()
        inv_row = inv_ref[...] * POINT_SCALE
        copies[0].wait()
        start = pl.multiple_of(layer * LANES, LANES)
        piece_ref[:LANES, :] = raw[pl.ds(start, LANES), :] * inv_row
        packed_ref[:rows, :] = raw[...] * inv_row
        copies[2].wait()
        for tile in range(tiles):
            packed_ref[rows + tile * columns : rows + (tile + 1) * columns, :] = raw_vectors[
                :, tile * LANES : (tile + 1) * LANES
            ]
        own_vectors = raw_vectors[:, pl.ds(start, LANES)]
        piece_ref[LANES:, :] = own_vectors
        copies[3].wait()
        term_ref[...] = own_vectors * noise_ref[...]

    outs = (
        ((rows + tiles * columns, feats), F32),
        ((LANES + columns, feats), F32),
        ((columns, LANES), F32),
    )
    scratch = (
        pltpu.VMEM((rows, feats), F32),
        pltpu.VMEM((columns, rows), F32),
        pltpu.VMEM((1, feats), F32),
        pltpu.VMEM((1, LANES), F32),
        pltpu.SemaphoreType.DMA((4,)),
    )
    return local_call(body, outs, (points, vectors_t, inv, noise), scratch, space=pltpu.HBM)


def load_left(packed, left, left_norms, left_vectors):
    rows = left.shape[0]
    columns = left_vectors.shape[0] // 2
    x = packed[:rows, :]
    left_norms[...] = jnp.broadcast_to(jnp.sum(x * x, axis=1, keepdims=True), (rows, LANES))
    high, middle, low = three_parts(x * (-2.0))
    feats = x.shape[1]
    for place, part in enumerate((high, middle, high, middle, high, low)):
        left[:, place * feats : (place + 1) * feats] = part
    for tile in range(rows // LANES):
        high, low = two_parts(packed[rows + tile * columns : rows + (tile + 1) * columns, :])
        left_vectors[:columns, tile * LANES : (tile + 1) * LANES] = high
        left_vectors[columns:, tile * LANES : (tile + 1) * LANES] = low


def load_right(pieces):
    held = [piece[...] for piece in pieces]
    y = stacked(*(piece[:LANES] for piece in held))
    right_norms = jnp.sum((y * y).T, axis=0, keepdims=True)
    high, middle, low = three_parts(y)
    right = side_by_side(high, high, middle, middle, low, high)
    high, low = two_parts(side_by_side(*(piece[LANES:] for piece in held)))
    right_vectors = side_by_side(stacked(high, low), stacked(high, jnp.zeros_like(high)))
    return right, right_norms, right_vectors


def tile_products(side, loaded, total_in, total, mirrored, backs):
    left, left_norms, left_vectors = side
    right, right_norms, right_vectors = loaded
    rows = left.shape[0]
    columns = left_vectors.shape[0] // 2
    count = right.shape[0] // LANES
    zero = jnp.zeros((columns, CHUNK), BF16)
    for chunk in range(rows // CHUNK):
        here = pl.ds(chunk * CHUNK, CHUNK)
        cross = across(left[here, :], right)
        norms = left_norms[here, :]
        square = jnp.maximum(cross + side_by_side(*(norms,) * count) + right_norms, TINY)
        radius = square * lax.rsqrt(square)
        kernel = ((radius + ROOT_THREE) * radius + 1.0) * jnp.exp2(radius * EXP2_SCALE)
        high, low = two_parts(kernel)
        direct = across(side_by_side(high, low), right_vectors)
        total[here, :] = direct if total_in is None else total_in[here, :] + direct
        if backs == 0:
            continue
        wide = backs * LANES
        own = left_vectors[:columns, here]
        own_low = left_vectors[columns:, here]
        part = jnp.dot(
            stacked(side_by_side(own, own), side_by_side(own_low, zero)),
            stacked(high[:, :wide], low[:, :wide]),
            preferred_element_type=F32,
        )
        mirrored = part if mirrored is None else mirrored + part
    return mirrored


def folded(mirrored):
    columns = mirrored.shape[0] // 2
    return mirrored[:columns] + mirrored[columns:]


def write_turned(total, turned_ref):
    columns = total.shape[1] // 2
    for place in range(turned_ref.shape[0]):
        turned = total[place * LANES : (place + 1) * LANES, :].T
        turned_ref[place, :, :] = turned[:columns] + turned[columns:]


def macs_of(rows, feats, columns, count):
    return rows * count * LANES * (6 * feats + 8 * columns)


def side_shapes(rows, feats, columns):
    return (
        ((rows, 2 * columns), F32),
        ((rows, 6 * feats), BF16),
        ((rows, LANES), F32),
        ((2 * columns, rows), BF16),
    )


def first_sides(packed, other_packed, piece):
    feats = packed.shape[1]
    columns = piece.shape[0] - LANES
    rows = packed.shape[0] * LANES // (LANES + columns)

    def body(packed, other_packed, *refs):
        load_left(packed, *refs[:3])
        load_left(other_packed, *refs[3:])

    side = side_shapes(rows, feats, columns)[1:]
    out = local_call(body, side + side, (packed, other_packed))
    return out[:3], out[3:]


def near_tiles(own, other, piece, arrived):
    rows, columns = own[0].shape[0], own[2].shape[0] // 2

    def body(*refs):
        own_side, other_side = refs[:3], refs[3:6]
        piece, arrived, total, other_total, back_ref = refs[6:]
        loaded = load_right((arrived, piece))
        mirrored = tile_products(own_side, loaded, None, total, None, 1)
        mirrored = tile_products(other_side, loaded, None, other_total, mirrored, 1)
        back_ref[...] = folded(mirrored)

    total_shape = ((rows, 2 * columns), F32)
    outs = (total_shape, total_shape, ((columns, LANES), F32))
    macs = macs_of(2 * rows, own[0].shape[1] // 6, columns, 2)
    return local_call(body, outs, (*own, *other, piece, arrived), macs=macs)


def other_tiles(side, pieces):
    rows, columns = side[1].shape[0], side[3].shape[0] // 2

    def body(*refs):
        (total_in, *side), arrived, turned_ref, part_ref, total = refs[:4], refs[4:7], *refs[7:]
        part_ref[...] = tile_products(side, load_right(arrived), total_in, total, None, 2)
        write_turned(total, turned_ref)

    outs = (((rows // LANES, columns, LANES), F32), ((2 * columns, 2 * LANES), F32))
    scratch = (pltpu.VMEM((rows, 2 * columns), F32),)
    macs = macs_of(rows, side[1].shape[1] // 6, columns, 2)
    return local_call(body, outs, (*side, *pieces), scratch, macs=macs)


def own_tiles(side, part, pieces):
    rows, columns = side[1].shape[0], side[3].shape[0] // 2

    def body(*refs):
        (total_in, *side), part_ref, arrived = refs[:4], refs[4], refs[5:7]
        total, first_ref, second_ref = refs[7:]
        loaded = load_right(arrived)
        mirrored = folded(tile_products(side, loaded, total_in, total, part_ref[...], 2))
        first_ref[...] = mirrored[:, :LANES]
        second_ref[...] = mirrored[:, LANES:]

    back = ((columns, LANES), F32)
    outs = (((rows, 2 * columns), F32), back, back)
    macs = macs_of(rows, side[1].shape[1] // 6, columns, 3)
    return local_call(body, outs, (*side, part, *pieces), macs=macs)


def joined(total, from_other):
    def body(total, from_other, tiles):
        write_turned(total, tiles)
        tiles[...] += from_other[...]

    return local_call(body, ((from_other.shape, F32),), (total, from_other))[0]


def per_device(points, inv_scale, vectors, noise):
    layers = lax.axis_size("layer")
    rows = points.shape[0]
    packed, piece, noise_term = prepare(points, inv_scale[None, :], vectors.T, noise[None, :])
    near, middle, far = CHIP_STEPS
    near_piece = stepped(piece, near)
    other_packed = swapped(packed)
    middle_piece = stepped(piece, middle)
    far_piece = stepped(piece, far)
    ring_piece = across_the_ring(piece)
    own, other = first_sides(packed, other_packed, piece)
    total, other_total, near_back = near_tiles(own, other, piece, near_piece)
    pieces = (middle_piece, far_piece)
    for_other, part = other_tiles((other_total, *other), (*pieces, ring_piece))
    from_other = swapped(for_other)
    total, middle_back, far_back = own_tiles((total, *own), part, pieces)
    tiles = lax.all_to_all(joined(total, from_other), "layer", 0, 0, tiled=True)
    returned = (
        stepped(near_back, -near) + stepped(middle_back, -middle) + stepped(far_back, -far)
    )
    normalizer = float(rows * (2 * layers - 1)) ** (-0.5)
    return ((jnp.sum(tiles, axis=0) + returned) * normalizer + noise_term).T


def solution(mesh):
    placed = (P("blk", None), P(), P("blk", None), P(("blk", "layer")))
    return jax.shard_map(
        per_device, mesh=mesh, in_specs=placed, out_specs=P(("blk", "layer"), None), check_vma=False
    )
```

```python
import jax
import jax.numpy as jnp
from jax import lax
from jax.experimental import pallas as pl
from jax.experimental.pallas import tpu as pltpu
from jax.sharding import PartitionSpec as P

F32 = jnp.float32
BF16 = jnp.bfloat16
ROOT_THREE = 3.0**0.5
POINT_SCALE = (5.0 / 3.0) ** 0.5
EXP2_SCALE = -ROOT_THREE * 1.4426950408889634
TINY = 1e-30
LANES = 128
CHUNK = 256
VMEM_BYTES = 32 * 1024 * 1024

NEAR = lambda x, y: (x, y + 1)
MIDDLE = lambda x, y: (x + 1, y - 1)
FAR = lambda x, y: (x + (y >= 2), y + 2)
ACROSS = lambda x, y: (x + 1, y)


def permuted(value, pairs, back=False):
    if back:
        pairs = [(target, source) for source, target in pairs]
    return lax.ppermute(value, "blk", pairs)


def swapped(value):
    return permuted(value, [(block, block ^ 1) for block in range(lax.axis_size("blk"))])


def stepped(value, step, back=False):
    half = lax.axis_size("blk") // 2
    pairs = []
    for block in range(2 * half):
        x, y = step(block // half, block % half // 2)
        pairs.append((block, x % 2 * half + y % (half // 2) * 2 + block % 2))
    return permuted(value, pairs, back)


def two_parts(x):
    high = x.astype(BF16)
    return high, (x - high.astype(F32)).astype(BF16)


def three_parts(x):
    high = x.astype(BF16)
    rest = x - high.astype(F32)
    middle = rest.astype(BF16)
    return high, middle, (rest - middle.astype(F32)).astype(BF16)


def side_by_side(*parts):
    return jnp.concatenate(parts, axis=1)


def stacked(*parts):
    return jnp.concatenate(parts, axis=0)


def across(left, right):
    return lax.dot_general(left, right, (((1,), (1,)), ((), ())), preferred_element_type=F32)


def local_call(body, outs, args, scratch=(), aliases=None, macs=0, space=pltpu.VMEM):
    whole = pl.BlockSpec(memory_space=pltpu.VMEM)
    return pl.pallas_call(
        body,
        out_shape=tuple(jax.ShapeDtypeStruct(shape, kind) for shape, kind in outs),
        in_specs=[pl.BlockSpec(memory_space=space)] * len(args),
        out_specs=(whole,) * len(outs),
        scratch_shapes=list(scratch),
        input_output_aliases=aliases or {},
        compiler_params=pltpu.CompilerParams(vmem_limit_bytes=VMEM_BYTES),
        cost_estimate=pl.CostEstimate(flops=2 * macs, bytes_accessed=1 << 20, transcendentals=0),
    )(*(pltpu.with_memory_space_constraint(arg, space) for arg in args))


def prepare(points, inv, vectors_t, noise):
    rows, feats = points.shape
    columns = vectors_t.shape[0]
    tiles = rows // LANES

    def body(
        points_hbm, vectors_hbm, inv_hbm, noise_hbm, packed_ref, piece_ref, term_ref,
        raw, raw_vectors, inv_ref, noise_ref, sems,
    ):
        layer = lax.axis_index("layer")
        copies = [
            pltpu.make_async_copy(source, target, sems.at[which])
            for which, (source, target) in enumerate(
                (
                    (points_hbm, raw),
                    (inv_hbm, inv_ref),
                    (vectors_hbm, raw_vectors),
                    (noise_hbm, noise_ref),
                )
            )
        ]
        for copy in copies:
            copy.start()
        copies[1].wait()
        inv_row = inv_ref[...] * POINT_SCALE
        copies[0].wait()
        start = pl.multiple_of(layer * LANES, LANES)
        piece_ref[:LANES, :] = raw[pl.ds(start, LANES), :] * inv_row
        packed_ref[:rows, :] = raw[...] * inv_row
        copies[2].wait()
        for tile in range(tiles):
            packed_ref[rows + tile * columns : rows + (tile + 1) * columns, :] = raw_vectors[
                :, tile * LANES : (tile + 1) * LANES
            ]
        own_vectors = raw_vectors[:, pl.ds(start, LANES)]
        piece_ref[LANES:, :] = own_vectors
        copies[3].wait()
        term_ref[...] = own_vectors * noise_ref[...]

    outs = (
        ((rows + tiles * columns, feats), F32),
        ((LANES + columns, feats), F32),
        ((columns, LANES), F32),
    )
    scratch = (
        pltpu.VMEM((rows, feats), F32),
        pltpu.VMEM((columns, rows), F32),
        pltpu.VMEM((1, feats), F32),
        pltpu.VMEM((1, LANES), F32),
        pltpu.SemaphoreType.DMA((4,)),
    )
    return local_call(body, outs, (points, vectors_t, inv, noise), scratch, space=pltpu.HBM)


def load_left(packed, left, left_norms, left_vectors):
    rows = left.shape[0]
    columns = left_vectors.shape[0] // 2
    x = packed[:rows, :]
    left_norms[...] = jnp.broadcast_to(jnp.sum(x * x, axis=1, keepdims=True), (rows, LANES))
    high, middle, low = three_parts(x * (-2.0))
    feats = x.shape[1]
    for place, part in enumerate((high, middle, high, middle, high, low)):
        left[:, place * feats : (place + 1) * feats] = part
    for tile in range(rows // LANES):
        high, low = two_parts(packed[rows + tile * columns : rows + (tile + 1) * columns, :])
        left_vectors[:columns, tile * LANES : (tile + 1) * LANES] = high
        left_vectors[columns:, tile * LANES : (tile + 1) * LANES] = low


def load_right(pieces):
    held = [piece[...] for piece in pieces]
    y = stacked(*(piece[:LANES] for piece in held))
    right_norms = jnp.sum((y * y).T, axis=0, keepdims=True)
    high, middle, low = three_parts(y)
    right = side_by_side(high, high, middle, middle, low, high)
    high, low = two_parts(side_by_side(*(piece[LANES:] for piece in held)))
    right_vectors = side_by_side(stacked(high, low), stacked(high, jnp.zeros_like(high)))
    return right, right_norms, right_vectors


def tile_products(side, loaded, total_in, total, mirrored, backs):
    left, left_norms, left_vectors = side
    right, right_norms, right_vectors = loaded
    rows = left.shape[0]
    columns = left_vectors.shape[0] // 2
    count = right.shape[0] // LANES
    zero = jnp.zeros((columns, CHUNK), BF16)
    for chunk in range(rows // CHUNK):
        here = pl.ds(chunk * CHUNK, CHUNK)
        cross = across(left[here, :], right)
        norms = left_norms[here, :]
        square = jnp.maximum(cross + side_by_side(*(norms,) * count) + right_norms, TINY)
        radius = square * lax.rsqrt(square)
        kernel = ((radius + ROOT_THREE) * radius + 1.0) * jnp.exp2(radius * EXP2_SCALE)
        high, low = two_parts(kernel)
        direct = across(side_by_side(high, low), right_vectors)
        total[here, :] = direct if total_in is None else total_in[here, :] + direct
        if backs == 0:
            continue
        wide = backs * LANES
        own = left_vectors[:columns, here]
        own_low = left_vectors[columns:, here]
        part = jnp.dot(
            stacked(side_by_side(own, own), side_by_side(own_low, zero)),
            stacked(high[:, :wide], low[:, :wide]),
            preferred_element_type=F32,
        )
        mirrored = part if mirrored is None else mirrored + part
    return mirrored


def folded(mirrored):
    columns = mirrored.shape[0] // 2
    return mirrored[:columns] + mirrored[columns:]


def write_turned(total, turned_ref):
    columns = total.shape[1] // 2
    for place in range(turned_ref.shape[0]):
        turned = total[place * LANES : (place + 1) * LANES, :].T
        turned_ref[place, :, :] = turned[:columns] + turned[columns:]


def macs_of(rows, feats, columns, count):
    return rows * count * LANES * (6 * feats + 8 * columns)


def side_shapes(rows, feats, columns):
    return (
        ((rows, 2 * columns), F32),
        ((rows, 6 * feats), BF16),
        ((rows, LANES), F32),
        ((2 * columns, rows), BF16),
    )


def first_sides(packed, other_packed, columns):
    feats = packed.shape[1]
    rows = packed.shape[0] * LANES // (LANES + columns)

    def body(packed, other_packed, *refs):
        load_left(packed, *refs[:3])
        load_left(other_packed, *refs[3:])

    side = side_shapes(rows, feats, columns)[1:]
    out = local_call(body, side + side, (packed, other_packed))
    return out[:3], out[3:]


def near_tiles(own, other, piece, arrived):
    rows, columns = own[0].shape[0], own[2].shape[0] // 2

    def body(*refs):
        own_side, other_side = refs[:3], refs[3:6]
        piece, arrived, total, other_total, back_ref = refs[6:]
        loaded = load_right((arrived, piece))
        mirrored = tile_products(own_side, loaded, None, total, None, 1)
        mirrored = tile_products(other_side, loaded, None, other_total, mirrored, 1)
        back_ref[...] = folded(mirrored)

    total_shape = ((rows, 2 * columns), F32)
    outs = (total_shape, total_shape, ((columns, LANES), F32))
    macs = macs_of(2 * rows, own[0].shape[1] // 6, columns, 2)
    return local_call(body, outs, (*own, *other, piece, arrived), macs=macs)


def middle_tile(side, piece):
    rows, columns = side[1].shape[0], side[3].shape[0] // 2

    def body(*refs):
        (total_in, *side), arrived, total, part_ref = refs[:4], *refs[4:]
        part_ref[...] = tile_products(side, load_right((arrived,)), total_in, total, None, 1)

    outs = (((rows, 2 * columns), F32), ((2 * columns, LANES), F32))
    macs = macs_of(rows, side[1].shape[1] // 6, columns, 1)
    return local_call(body, outs, (*side, piece), macs=macs)


def other_tiles(side, pieces):
    rows, columns = side[1].shape[0], side[3].shape[0] // 2

    def body(*refs):
        (total_in, *side), arrived, turned_ref, part_ref, total = refs[:4], refs[4:6], *refs[6:]
        part_ref[...] = tile_products(side, load_right(arrived), total_in, total, None, 1)
        write_turned(total, turned_ref)

    outs = (((rows // LANES, columns, LANES), F32), ((2 * columns, LANES), F32))
    scratch = (pltpu.VMEM((rows, 2 * columns), F32),)
    macs = macs_of(rows, side[1].shape[1] // 6, columns, 2)
    return local_call(body, outs, (*side, *pieces), scratch, macs=macs)


def own_tiles(side, parts, pieces):
    rows, columns = side[1].shape[0], side[3].shape[0] // 2

    def body(*refs):
        (total_in, *side), parts, arrived = refs[:4], refs[4:6], refs[6:8]
        total, first_ref, second_ref = refs[8:]
        begun = side_by_side(parts[0][...], parts[1][...])
        mirrored = folded(tile_products(side, load_right(arrived), total_in, total, begun, 2))
        first_ref[...] = mirrored[:, :LANES]
        second_ref[...] = mirrored[:, LANES:]

    back = ((columns, LANES), F32)
    outs = (((rows, 2 * columns), F32), back, back)
    macs = macs_of(rows, side[1].shape[1] // 6, columns, 2)
    return local_call(body, outs, (*side, *parts, *pieces), macs=macs)


def joined(total, from_other):
    def body(total, from_other, tiles):
        write_turned(total, tiles)
        tiles[...] += from_other[...]

    return local_call(body, ((from_other.shape, F32),), (total, from_other))[0]


def per_device(points, inv_scale, vectors, noise):
    layers = lax.axis_size("layer")
    rows = points.shape[0]
    packed, piece, noise_term = prepare(points, inv_scale[None, :], vectors.T, noise[None, :])
    near_piece = stepped(piece, NEAR)
    other_packed = swapped(packed)
    middle_piece = stepped(piece, MIDDLE)
    far_piece = stepped(piece, FAR)
    ring_piece = stepped(piece, ACROSS)
    own, other = first_sides(packed, other_packed, vectors.shape[1])
    total, other_total, near_back = near_tiles(own, other, piece, near_piece)
    other_total, middle_part = middle_tile((other_total, *other), middle_piece)
    for_other, far_part = other_tiles((other_total, *other), (far_piece, ring_piece))
    from_other = swapped(for_other)
    parts, pieces = (middle_part, far_part), (middle_piece, far_piece)
    total, middle_back, far_back = own_tiles((total, *own), parts, pieces)
    tiles = lax.all_to_all(joined(total, from_other), "layer", 0, 0, tiled=True)
    returned = (
        stepped(near_back, NEAR, True) + stepped(middle_back, MIDDLE, True) + stepped(far_back, FAR, True)
    )
    normalizer = float(rows * (2 * layers - 1)) ** (-0.5)
    return ((jnp.sum(tiles, axis=0) + returned) * normalizer + noise_term).T


def solution(mesh):
    placed = (P("blk", None), P(), P("blk", None), P(("blk", "layer")))
    return jax.shard_map(
        per_device, mesh=mesh, in_specs=placed, out_specs=P(("blk", "layer"), None), check_vma=False
    )
```

```python
import jax
import jax.numpy as jnp
from jax import lax
from jax.experimental import pallas as pl
from jax.experimental.pallas import tpu as pltpu
from jax.sharding import PartitionSpec as P

F32 = jnp.float32
BF16 = jnp.bfloat16
ROOT_THREE = 3.0**0.5
POINT_SCALE = (5.0 / 3.0) ** 0.5
EXP2_SCALE = -ROOT_THREE * 1.4426950408889634
TINY = 1e-30
LANES = 128
CHUNK = 256
VMEM_BYTES = 32 * 1024 * 1024

NEAR = lambda x, y: (x, y + 1)
MIDDLE = lambda x, y: (x + 1, y - 1)
FAR = lambda x, y: (x + (y >= 2), y + 2)
ACROSS = lambda x, y: (x + 1, y)


def permuted(value, pairs, back=False):
    if back:
        pairs = [(target, source) for source, target in pairs]
    return lax.ppermute(value, "blk", pairs)


def swapped(value):
    return permuted(value, [(block, block ^ 1) for block in range(lax.axis_size("blk"))])


def stepped(value, step, back=False):
    half = lax.axis_size("blk") // 2
    pairs = []
    for block in range(2 * half):
        x, y = step(block // half, block % half // 2)
        pairs.append((block, x % 2 * half + y % (half // 2) * 2 + block % 2))
    return permuted(value, pairs, back)


def two_parts(x):
    high = x.astype(BF16)
    return high, (x - high.astype(F32)).astype(BF16)


def three_parts(x):
    high = x.astype(BF16)
    rest = x - high.astype(F32)
    middle = rest.astype(BF16)
    return high, middle, (rest - middle.astype(F32)).astype(BF16)


def side_by_side(*parts):
    return jnp.concatenate(parts, axis=1)


def stacked(*parts):
    return jnp.concatenate(parts, axis=0)


def across(left, right):
    return lax.dot_general(left, right, (((1,), (1,)), ((), ())), preferred_element_type=F32)


def local_call(body, outs, args, scratch=(), aliases=None, macs=0, space=pltpu.VMEM):
    whole = pl.BlockSpec(memory_space=pltpu.VMEM)
    return pl.pallas_call(
        body,
        out_shape=tuple(jax.ShapeDtypeStruct(shape, kind) for shape, kind in outs),
        in_specs=[pl.BlockSpec(memory_space=space)] * len(args),
        out_specs=(whole,) * len(outs),
        scratch_shapes=list(scratch),
        input_output_aliases=aliases or {},
        compiler_params=pltpu.CompilerParams(vmem_limit_bytes=VMEM_BYTES),
        cost_estimate=pl.CostEstimate(flops=2 * macs, bytes_accessed=1 << 20, transcendentals=0),
    )(*(pltpu.with_memory_space_constraint(arg, space) for arg in args))


def prepare(points, inv, vectors_t, noise):
    rows, feats = points.shape
    columns = vectors_t.shape[0]
    tiles = rows // LANES

    def body(
        points_hbm, vectors_hbm, inv_hbm, noise_hbm, packed_ref, piece_ref, term_ref,
        raw, raw_vectors, inv_ref, noise_ref, sems,
    ):
        layer = lax.axis_index("layer")
        copies = [
            pltpu.make_async_copy(source, target, sems.at[which])
            for which, (source, target) in enumerate(
                (
                    (points_hbm, raw),
                    (inv_hbm, inv_ref),
                    (vectors_hbm, raw_vectors),
                    (noise_hbm, noise_ref),
                )
            )
        ]
        for copy in copies:
            copy.start()
        copies[1].wait()
        inv_row = inv_ref[...] * POINT_SCALE
        copies[0].wait()
        start = pl.multiple_of(layer * LANES, LANES)
        piece_ref[:LANES, :] = raw[pl.ds(start, LANES), :] * inv_row
        packed_ref[:rows, :] = raw[...] * inv_row
        copies[2].wait()
        for tile in range(tiles):
            packed_ref[rows + tile * columns : rows + (tile + 1) * columns, :] = raw_vectors[
                :, tile * LANES : (tile + 1) * LANES
            ]
        own_vectors = raw_vectors[:, pl.ds(start, LANES)]
        piece_ref[LANES:, :] = own_vectors
        copies[3].wait()
        term_ref[...] = own_vectors * noise_ref[...]

    outs = (
        ((rows + tiles * columns, feats), F32),
        ((LANES + columns, feats), F32),
        ((columns, LANES), F32),
    )
    scratch = (
        pltpu.VMEM((rows, feats), F32),
        pltpu.VMEM((columns, rows), F32),
        pltpu.VMEM((1, feats), F32),
        pltpu.VMEM((1, LANES), F32),
        pltpu.SemaphoreType.DMA((4,)),
    )
    return local_call(body, outs, (points, vectors_t, inv, noise), scratch, space=pltpu.HBM)


def load_left(packed, left, left_norms, left_vectors):
    rows = left.shape[0]
    columns = left_vectors.shape[0] // 2
    x = packed[:rows, :]
    left_norms[...] = jnp.broadcast_to(jnp.sum(x * x, axis=1, keepdims=True), (rows, LANES))
    high, middle, low = three_parts(x * (-2.0))
    feats = x.shape[1]
    for place, part in enumerate((high, middle, high, middle, high, low)):
        left[:, place * feats : (place + 1) * feats] = part
    for tile in range(rows // LANES):
        high, low = two_parts(packed[rows + tile * columns : rows + (tile + 1) * columns, :])
        left_vectors[:columns, tile * LANES : (tile + 1) * LANES] = high
        left_vectors[columns:, tile * LANES : (tile + 1) * LANES] = low


def load_right(pieces):
    held = [piece[...] for piece in pieces]
    y = stacked(*(piece[:LANES] for piece in held))
    right_norms = jnp.sum((y * y).T, axis=0, keepdims=True)
    high, middle, low = three_parts(y)
    right = side_by_side(high, high, middle, middle, low, high)
    high, low = two_parts(side_by_side(*(piece[LANES:] for piece in held)))
    right_vectors = side_by_side(stacked(high, low), stacked(high, jnp.zeros_like(high)))
    return right, right_norms, right_vectors


def tile_products(side, loaded, total_in, total, mirrored, backs):
    left, left_norms, left_vectors = side
    right, right_norms, right_vectors = loaded
    rows = left.shape[0]
    columns = left_vectors.shape[0] // 2
    count = right.shape[0] // LANES
    zero = jnp.zeros((columns, CHUNK), BF16)
    for chunk in range(rows // CHUNK):
        here = pl.ds(chunk * CHUNK, CHUNK)
        cross = across(left[here, :], right)
        norms = left_norms[here, :]
        square = jnp.maximum(cross + side_by_side(*(norms,) * count) + right_norms, TINY)
        radius = square * lax.rsqrt(square)
        kernel = ((radius + ROOT_THREE) * radius + 1.0) * jnp.exp2(radius * EXP2_SCALE)
        high, low = two_parts(kernel)
        direct = across(side_by_side(high, low), right_vectors)
        total[here, :] = direct if total_in is None else total_in[here, :] + direct
        if backs == 0:
            continue
        wide = backs * LANES
        own = left_vectors[:columns, here]
        own_low = left_vectors[columns:, here]
        part = jnp.dot(
            stacked(side_by_side(own, own), side_by_side(own_low, zero)),
            stacked(high[:, :wide], low[:, :wide]),
            preferred_element_type=F32,
        )
        mirrored = part if mirrored is None else mirrored + part
    return mirrored


def folded(mirrored):
    columns = mirrored.shape[0] // 2
    return mirrored[:columns] + mirrored[columns:]


def write_turned(total, turned_ref):
    columns = total.shape[1] // 2
    for place in range(turned_ref.shape[0]):
        turned = total[place * LANES : (place + 1) * LANES, :].T
        turned_ref[place, :, :] = turned[:columns] + turned[columns:]


def macs_of(rows, feats, columns, count):
    return rows * count * LANES * (6 * feats + 8 * columns)


def side_shapes(rows, feats, columns):
    return (
        ((rows, 2 * columns), F32),
        ((rows, 6 * feats), BF16),
        ((rows, LANES), F32),
        ((2 * columns, rows), BF16),
    )


def near_tiles(packed, other_packed, piece, arrived):
    feats = packed.shape[1]
    columns = piece.shape[0] - LANES
    rows = packed.shape[0] * LANES // (LANES + columns)

    def body(packed, other_packed, piece, arrived, *refs):
        (total, *own), (other_total, *other), back_ref = refs[:4], refs[4:8], refs[8]
        load_left(packed, *own)
        load_left(other_packed, *other)
        loaded = load_right((arrived, piece))
        mirrored = tile_products(own, loaded, None, total, None, 1)
        mirrored = tile_products(other, loaded, None, other_total, mirrored, 1)
        back_ref[...] = folded(mirrored)

    side = side_shapes(rows, feats, columns)
    outs = side + side + (((columns, LANES), F32),)
    macs = macs_of(2 * rows, feats, columns, 2)
    out = local_call(body, outs, (packed, other_packed, piece, arrived), macs=macs)
    return out[:4], out[4:8], out[8]


def middle_tile(side, piece):
    rows, columns = side[1].shape[0], side[3].shape[0] // 2

    def body(*refs):
        (total_in, *side), arrived, total, part_ref = refs[:4], *refs[4:]
        part_ref[...] = tile_products(side, load_right((arrived,)), total_in, total, None, 1)

    outs = (((rows, 2 * columns), F32), ((2 * columns, LANES), F32))
    macs = macs_of(rows, side[1].shape[1] // 6, columns, 1)
    return local_call(body, outs, (*side, piece), macs=macs)


def other_tiles(side, pieces):
    rows, columns = side[1].shape[0], side[3].shape[0] // 2

    def body(*refs):
        (total_in, *side), arrived, turned_ref, part_ref, total = refs[:4], refs[4:6], *refs[6:]
        part_ref[...] = tile_products(side, load_right(arrived), total_in, total, None, 1)
        write_turned(total, turned_ref)

    outs = (((rows // LANES, columns, LANES), F32), ((2 * columns, LANES), F32))
    scratch = (pltpu.VMEM((rows, 2 * columns), F32),)
    macs = macs_of(rows, side[1].shape[1] // 6, columns, 2)
    return local_call(body, outs, (*side, *pieces), scratch, macs=macs)


def own_tiles(side, parts, pieces):
    rows, columns = side[1].shape[0], side[3].shape[0] // 2

    def body(*refs):
        (total_in, *side), parts, arrived = refs[:4], refs[4:6], refs[6:8]
        total, first_ref, second_ref = refs[8:]
        begun = side_by_side(parts[0][...], parts[1][...])
        mirrored = folded(tile_products(side, load_right(arrived), total_in, total, begun, 2))
        first_ref[...] = mirrored[:, :LANES]
        second_ref[...] = mirrored[:, LANES:]

    back = ((columns, LANES), F32)
    outs = (((rows, 2 * columns), F32), back, back)
    macs = macs_of(rows, side[1].shape[1] // 6, columns, 2)
    return local_call(body, outs, (*side, *parts, *pieces), macs=macs)


def joined(total, from_other):
    def body(total, from_other, tiles):
        write_turned(total, tiles)
        tiles[...] += from_other[...]

    return local_call(body, ((from_other.shape, F32),), (total, from_other))[0]


def per_device(points, inv_scale, vectors, noise):
    layers = lax.axis_size("layer")
    rows = points.shape[0]
    packed, piece, noise_term = prepare(points, inv_scale[None, :], vectors.T, noise[None, :])
    near_piece = stepped(piece, NEAR)
    other_packed = swapped(packed)
    middle_piece = stepped(piece, MIDDLE)
    far_piece = stepped(piece, FAR)
    ring_piece = stepped(piece, ACROSS)
    (total, *own), (other_total, *other), near_back = near_tiles(
        packed, other_packed, piece, near_piece
    )
    other_total, middle_part = middle_tile((other_total, *other), middle_piece)
    for_other, far_part = other_tiles((other_total, *other), (far_piece, ring_piece))
    from_other = swapped(for_other)
    parts, pieces = (middle_part, far_part), (middle_piece, far_piece)
    total, middle_back, far_back = own_tiles((total, *own), parts, pieces)
    tiles = lax.all_to_all(joined(total, from_other), "layer", 0, 0, tiled=True)
    returned = (
        stepped(near_back, NEAR, True) + stepped(middle_back, MIDDLE, True) + stepped(far_back, FAR, True)
    )
    normalizer = float(rows * (2 * layers - 1)) ** (-0.5)
    return ((jnp.sum(tiles, axis=0) + returned) * normalizer + noise_term).T


def solution(mesh):
    placed = (P("blk", None), P(), P("blk", None), P(("blk", "layer")))
    return jax.shard_map(
        per_device, mesh=mesh, in_specs=placed, out_specs=P(("blk", "layer"), None), check_vma=False
    )
```
